512 devices in a mesh: rep: 8 (over x, core), dp: 8 (over z), expert: 8 (over y).
Axes of the slice: x: 4, y: 8, z: 8, core: 2. Of those that a mesh axis runs over, the one named last changes fastest.
Arguments:
- layer_out: bfloat16 [8192, 4096], P(('dp', 'expert'), 'rep'), may hold values from -6 to 6
- frozen_out: bfloat16 [8192, 4096], P(('dp', 'expert'), 'rep'), may hold values from -6 to 6
- control: float32 [4096], P('rep'), may hold values from -6 to 6
- row_kind: int32 [8192], P(('dp', 'expert')), may hold values 0 or 1
- expert_ids: int32 [8192, 2], P(('dp', 'expert')), may hold values from 0 to 7, all different within a row; in each aligned block of 128 rows (0 to 127, 128 to 255, ...) at most 48 rows name the same one
- route_weights: float32 [8192, 2], P(('dp', 'expert')), may hold values from 0.2 to 1
- hidden: bfloat16 [8, 3072, 14336], P('expert', 'rep', 'dp'), may hold values from -6 to 6
Outputs:
- grad_down: float32 [8, 14336, 4096], P('expert', 'dp', 'rep')
The draws below stay inside these ranges and needn't reach their ends.
Inputs may be any that keep to these rules, and one draw needn't show every extreme that they name: `expert_ids`: each token names two different experts; among the 128 tokens of one index of dp and expert no expert is named more than 48 times, and in every draw some expert of some such block is named exactly 48 times.
All inputs are finite; a program needn't handle non-finite values. No bound on the sum of `row_kind` on one device may be relied on, other than what follows from the above.
Results may differ from the reference program's by a relative error of at most 0.0029.
Values may be sent and summed in bfloat16 or wider, within the bound.
No kernel may reach another device: no remote copies, remote signals or barrier semaphores. Data moves between devices by JAX's collectives and lax.ppermute only.
A program may use at most 64 MiB of HBM per device.

```python
import math
import jax
import jax.numpy as jnp
import numpy as np
from jax import lax

D = 4096
NEXP = 8
FFW = 14336
TOK_DEV = 128
CAP = 48
TOKENS = 8192
ROWS_EXP = 3072


def set_ends(drawn, own_key, least, largest):
    spot = [jax.random.randint(jax.random.fold_in(own_key, axis), (), 0, length) for axis, length in enumerate(drawn.shape)]
    longest = drawn.shape.index(max(drawn.shape))
    next_to = spot[:longest] + [(spot[longest] + 1) % drawn.shape[longest]] + spot[longest + 1:]
    return drawn.at[tuple(spot)].set(least).at[tuple(next_to)].set(largest)


def shard_levels(stream_key, shape, cuts, low, top_value):
    level, own = 1.0, jax.random.fold_in(stream_key, 6)
    for dim, parts in cuts:
        steps = jnp.exp(jax.random.uniform(jax.random.fold_in(own, dim), (parts,), jnp.float32, low / len(cuts), top_value / len(cuts)))
        level = level * jnp.repeat(steps, shape[dim] // parts).reshape([-1 if axis == dim else 1 for axis in range(len(shape))])
    return level


def shared_out(rng, own, number, rows, count, top, limit, slope):
    ranking = jax.random.permutation(rng, count)
    heavy_load, ordinary = portions_of(count, rows * top, limit, slope, True), portions_of(count, rows * top, limit, slope, False)
    places = jnp.arange(count)

    def named(lengths, offset_by):
        used = int((lengths > 0).sum())
        fixed = max(1, used // 4)
        moved = fixed + (places - fixed + offset_by * (used - fixed)) % max(1, count - fixed)
        return jnp.zeros((count,), jnp.int32).at[ranking[jnp.where(places < fixed, places, moved)]].set(jnp.asarray(lengths, jnp.int32))

    lengths = jnp.where(number % 4 == 0, named(heavy_load, number // 4), named(ordinary, number - number // 4 - 1))
    mixed = jax.random.permutation(jax.random.fold_in(own, 3), count)
    donor, taker = mixed[0:count // 2 * 2:2], mixed[1:count // 2 * 2:2]
    slack = jnp.minimum(lengths[donor] - 1, limit - lengths[taker]) // 2
    slack = jnp.where((donor == ranking[0]) | (taker == ranking[0]) | (lengths[taker] == 0), 0, jnp.maximum(slack, 0))
    moved = jax.random.randint(jax.random.fold_in(own, 4), (count // 2,), 0, 1 << 20) % (slack + 1)
    lengths = lengths.at[donor].add(-moved).at[taker].add(moved)
    items = jnp.searchsorted(jnp.cumsum(lengths), jnp.arange(rows * top), side="right").astype(jnp.int32)
    listing = items.reshape(top, rows).T
    listing = listing[jax.random.permutation(jax.random.fold_in(own, 1), rows)]
    offset_by = jax.random.randint(jax.random.fold_in(own, 2), (rows, 1), 0, top)
    return jnp.take_along_axis(listing, (jnp.arange(top)[None, :] + offset_by) % top, axis=1)


def portions_of(count, total, most, skew, full):
    weights = [(1 << 20) // math.isqrt(grade ** skew) + 1 for grade in range(1, count + 1)]
    largest = most if full else min(most, max(-(-total // count), total * weights[0] // sum(weights)))
    least = 1 if total - largest >= count - 1 else 0
    counts, surplus = [largest] + [least] * (count - 1), total - largest - least * (count - 1)
    while surplus > 0:
        candidates = [i for i in range(1, count) if counts[i] < largest] or [i for i in range(1, count) if counts[i] < most]
        pool, budget = sum([weights[i] for i in candidates]), surplus
        for i in candidates:
            addition = min(most - counts[i], max(1, budget * weights[i] // pool), surplus)
            counts[i] = counts[i] + addition
            surplus = surplus - addition
    return np.array(counts)


def normal_values(rng, shape, width, most, pieces=(), kind=jnp.bfloat16):
    result = width * jax.random.normal(rng, shape, jnp.float32)
    if pieces:
        result = result * shard_levels(rng, shape, pieces, -0.22, 0.18)
    return jnp.clip(result, -most, most).astype(kind)


def setup_inputs(seed: int = 0) -> dict:
    arg_keys = jax.random.split(jax.random.key(seed), 8)
    layer_out = normal_values(arg_keys[0], (TOKENS, D), 1.0, 6.0, ((0, 64), (1, 8)))
    frozen_out = normal_values(arg_keys[1], (TOKENS, D), 1.0, 6.0, ((0, 64), (1, 8)))
    control = normal_values(arg_keys[2], (D,), 1.0, 6.0, ((0, 8),), jnp.float32)
    row_kind = set_ends((jax.random.randint(arg_keys[3], (TOKENS,), 0, 2) < 1).astype(jnp.int32), jax.random.fold_in(arg_keys[3], 1), 0, 1)
    expert_ids_keys = jax.random.split(jax.random.fold_in(arg_keys[4], 1), TOKENS // TOK_DEV)
    expert_ids_turns = jax.random.permutation(jax.random.fold_in(arg_keys[4], 3), TOKENS // TOK_DEV)
    expert_ids = jax.vmap(lambda own, number: shared_out(jax.random.fold_in(arg_keys[4], 2), own, number, TOK_DEV, NEXP, 2, CAP, 2))(expert_ids_keys, expert_ids_turns).reshape((TOKENS, 2))
    route_weights = jnp.clip(0.2 + 0.8 * jax.random.uniform(arg_keys[5], (TOKENS, 2), jnp.float32) ** shard_levels(arg_keys[5], (TOKENS, 2), ((0, 64),), -0.2, 0.2), 0.2, 1.0)
    hidden = normal_values(arg_keys[6], (NEXP, ROWS_EXP, FFW), 1.0, 6.0, ((0, 8), (1, 8), (2, 8)))
    return {"layer_out": layer_out, "frozen_out": frozen_out, "control": control, "row_kind": row_kind, "expert_ids": expert_ids, "route_weights": route_weights, "hidden": hidden}


retain_weight = 2.0

def weight_grad(operands):
    hidden_rows, grad_rows = operands
    return jnp.dot(hidden_rows.T, grad_rows, preferred_element_type=jnp.float32)

def reference(layer_out, frozen_out, control, row_kind, expert_ids, route_weights, hidden):
    blocks = TOKENS // TOK_DEV
    route_ids = expert_ids.reshape(blocks, TOK_DEV * 2)
    matches = (route_ids[:, :, None] == jnp.arange(NEXP, dtype=jnp.int32)[None, None, :]).astype(jnp.int32)
    before = jnp.cumsum(matches, axis=1) - matches
    slot_idx = lax.optimization_barrier(jnp.sum(before * matches, axis=2)).reshape(TOKENS, 2)
    block_of = (jnp.arange(TOKENS, dtype=jnp.int32) // TOK_DEV)[:, None]
    position = (block_of * CAP + slot_idx).astype(jnp.int32)
    retain = (row_kind == 1)[:, None]
    target = jnp.where(retain, frozen_out.astype(jnp.float32), control[None, :])
    row_scale = jnp.where(retain, jnp.float32(retain_weight), jnp.float32(1.0))
    out_grad = row_scale * (layer_out.astype(jnp.float32) - target) * (1.0 / math.sqrt(TOKENS))
    grad_send = route_weights[:, :, None] * out_grad[:, None, :]
    grad_buffer = jnp.zeros((NEXP, blocks * CAP, D), jnp.float32).at[expert_ids, position].set(grad_send)
    grad_buffer = grad_buffer.astype(jnp.bfloat16)
    return lax.map(weight_grad, (hidden, grad_buffer))
```

```python
import math

import jax
import jax.numpy as jnp
from jax import lax
from jax.experimental import pallas as pl
from jax.experimental.pallas import tpu as pltpu
from jax.sharding import PartitionSpec as P

retain_weight = 2.0
tile = 256
split = 768


def ring(count, step, stride=1):
    return [(i, (i + step * stride) % count) for i in range(count)]


def outgoing_rows(layer_out, frozen_out, control, row_kind, expert_ids, route_weights, experts_all, total_tokens):
    tok_rows, feat_cols = layer_out.shape
    capacity = tok_rows * 3 // 8
    flat_ids = expert_ids.reshape(-1)
    matches = (flat_ids[:, None] == jnp.arange(experts_all, dtype=jnp.int32)[None, :]).astype(jnp.int32)
    before = jnp.cumsum(matches, axis=0) - matches
    slot_idx = jnp.sum(before * matches, axis=1)
    column_idx = flat_ids * capacity + slot_idx
    columns = jnp.arange(experts_all * capacity, dtype=jnp.int32)
    placed = (
        (column_idx[:, None] == columns[None, :])
        .astype(jnp.float32)
        .reshape(tok_rows, 2, experts_all * capacity)
    )
    weighted = jnp.sum(placed * route_weights[:, :, None], axis=1)
    retain = (row_kind == 1)[:, None]
    target = jnp.where(retain, frozen_out.astype(jnp.float32), control[None, :])
    row_scale = jnp.where(retain, jnp.float32(retain_weight), jnp.float32(1.0))
    out_grad = row_scale * (layer_out.astype(jnp.float32) - target) * (1.0 / math.sqrt(total_tokens))
    rows = jnp.dot(weighted.T, out_grad, precision=lax.Precision.HIGHEST)
    return rows.reshape(experts_all, capacity, feat_cols).astype(jnp.bfloat16)


def product_kernel(place_ref, own_a, other_a, own_b0, own_b1, own_b2, own_b3, oth_b0, oth_b1, oth_b2, oth_b3,
                   g0, r1, l1, r2, l2, r3, l3, r4, l4, out_ref, rows_a, rows_b, *, tiles_a):
    step = pl.program_id(0)
    block, cols = g0.shape
    half = block // 2

    @pl.when(step == 0)
    def _():
        rep, dp = place_ref[0], place_ref[1]
        chip, core = rep // 2, lax.rem(rep, 2)

        def put(piece, offset, start, size):
            slot_block = lax.rem(dp + offset + 8, 8)
            from_chip, from_core = slot_block // 2, lax.rem(slot_block, 2)
            group = jnp.where(from_core == core, 0, 4)
            hop = jnp.where(from_core == 0, lax.rem(chip - from_chip + 4, 4), lax.rem(from_chip - chip + 4, 4))
            rows_a[pl.ds(pl.multiple_of((group + from_chip) * block + start, half), size), :] = piece[...]
            rows_b[pl.ds(pl.multiple_of((group + hop) * block + start, half), size), :] = piece[...]

        put(g0, 0, 0, block)
        put(r1, -1, 0, block)
        put(l1, 1, 0, block)
        put(r2, -2, 0, block)
        put(l2, 2, 0, block)
        put(r3, -3, 0, block)
        put(l3, 3, 0, block)
        put(r4, -4, 0, half)
        put(l4, 4, half, half)

    contract = (((0,), (0,)), ((), ()))

    @pl.when(step < tiles_a)
    def _():
        slots = jnp.concatenate([own_a[k] for k in range(4)] + [other_a[k] for k in range(4)], axis=0)
        out_ref[...] = lax.dot_general(slots, rows_a[...], contract, preferred_element_type=jnp.float32)

    @pl.when(step >= tiles_a)
    def _():
        slots = jnp.concatenate(
            [p[...] for p in (own_b0, own_b1, own_b2, own_b3, oth_b0, oth_b1, oth_b2, oth_b3)], axis=0
        )
        out_ref[...] = lax.dot_general(slots, rows_b[...], contract, preferred_element_type=jnp.float32)


def product(place, own_a, other_a, own_b, other_b, pieces):
    block, cols = pieces[0].shape
    tiles_a, tiles_b = own_a.shape[2] // tile, own_b[0].shape[1] // tile

    def at_a(i):
        return (0, 0, jnp.minimum(i, tiles_a - 1))

    def at_b(i):
        return (0, jnp.maximum(i - tiles_a, 0))

    in_specs = [pl.BlockSpec(memory_space=pltpu.SMEM)]
    in_specs += [pl.BlockSpec((4, block, tile), at_a)] * 2
    in_specs += [pl.BlockSpec((block, tile), at_b)] * 8
    in_specs += [
        pl.BlockSpec(p.shape, lambda i: (0, 0), pipeline_mode=pl.Buffered(1)) for p in pieces
    ]
    width = tile * (tiles_a + tiles_b)
    return pl.pallas_call(
        lambda *refs: product_kernel(*refs, tiles_a=tiles_a),
        grid=(tiles_a + tiles_b,),
        in_specs=in_specs,
        out_specs=pl.BlockSpec((tile, cols), lambda i: (i, 0)),
        out_shape=jax.ShapeDtypeStruct((width, cols), jnp.float32),
        scratch_shapes=[pltpu.VMEM((8 * block, cols), jnp.bfloat16)] * 2,
        compiler_params=pltpu.CompilerParams(vmem_limit_bytes=40 * 2**20),
        cost_estimate=pl.CostEstimate(
            flops=2 * 8 * block * cols * width, bytes_accessed=8 * block * (cols + width) * 2 + width * cols * 4, transcendentals=0
        ),
    )(place, own_a, other_a, *own_b, *other_b, *pieces)


def body(layer_out, frozen_out, control, row_kind, expert_ids, route_weights, hidden):
    exp_local, slots, width = hidden.shape
    dp_count = lax.axis_size("dp")
    exp_count = lax.axis_size("expert")
    total_tokens = layer_out.shape[0] * dp_count * exp_count
    held = hidden.reshape(slots, width)
    part_a, part_b = held[:, :split], held[:, split:]

    cores = [(i, i ^ 1) for i in range(8)]
    round_chips = [(2 * x + c, 2 * ((x + (1, -1)[c]) % 4) + c) for x in range(4) for c in range(2)]
    own_b = [part_b]
    for _ in range(3):
        own_b.append(lax.ppermute(own_b[-1], "rep", round_chips))
    other_b = [lax.ppermute(p, "rep", cores) for p in own_b]

    own_a = lax.all_to_all(
        jnp.broadcast_to(part_a[None], (4,) + part_a.shape), "rep", split_axis=0, concat_axis=0, tiled=True,
        axis_index_groups=[[0, 2, 4, 6], [1, 3, 5, 7]],
    )
    other_a = lax.ppermute(own_a, "rep", cores)

    grad_send = outgoing_rows(
        layer_out, frozen_out, control, row_kind, expert_ids, route_weights, exp_local * exp_count, total_tokens
    )
    mine = lax.all_to_all(grad_send, "expert", split_axis=0, concat_axis=0, tiled=True)
    mine = mine.reshape(-1, mine.shape[2])
    half = mine.shape[0] // 2
    pieces = [mine]
    right = left = mine
    for _ in range(3):
        right = lax.ppermute(right, "dp", ring(8, 1))
        left = lax.ppermute(left, "dp", ring(8, -1))
        pieces += [right, left]
    pieces.append(lax.ppermute(right[:half], "dp", ring(8, 1)))
    pieces.append(lax.ppermute(left[half:], "dp", ring(8, -1)))

    place = jnp.stack([lax.axis_index("rep"), lax.axis_index("dp")]).astype(jnp.int32)
    return product(place, own_a, other_a, own_b, other_b, pieces)[None]


def solution(mesh):
    in_specs = (
        P(("dp", "expert"), "rep"),
        P(("dp", "expert"), "rep"),
        P("rep"),
        P(("dp", "expert")),
        P(("dp", "expert"), None),
        P(("dp", "expert"), None),
        P("expert", "rep", "dp"),
    )
    out_specs = P("expert", "dp", "rep")
    return jax.shard_map(body, mesh=mesh, in_specs=in_specs, out_specs=out_specs, check_vma=False)
```

```python
import math

import jax
import jax.numpy as jnp
from jax import lax
from jax.experimental import pallas as pl
from jax.experimental.pallas import tpu as pltpu
from jax.sharding import PartitionSpec as P

retain_weight = 2.0
tile = 256


def rows_kernel(lo_ref, fr_ref, control_ref, kind_ref, ids_ref, weights_ref, out_ref, *, experts, scale):
    tokens, feats = lo_ref.shape
    capacity = out_ref.shape[0] // experts
    down = lax.broadcasted_iota(jnp.int32, (tokens, tokens), 0)
    across = lax.broadcasted_iota(jnp.int32, (tokens, tokens), 1)
    earlier = (down < across).astype(jnp.float32)
    expert = lax.broadcasted_iota(jnp.int32, (experts, tokens), 0)
    first, second = ids_ref[0:1, :] == expert, ids_ref[1:2, :] == expert
    named = (first | second).astype(jnp.float32)
    weight = jnp.where(first, weights_ref[0:1, :], 0.0) + jnp.where(second, weights_ref[1:2, :], 0.0)
    slot = jnp.dot(named, earlier, preferred_element_type=jnp.float32).astype(jnp.int32)
    slot = jnp.where(first | second, slot, -1)
    wanted = lax.broadcasted_iota(jnp.int32, (experts, capacity, tokens), 1)
    placed = jnp.where(slot[:, None, :] == wanted, weight[:, None, :], 0.0)
    placed = placed.reshape(experts * capacity, tokens)
    kind = jnp.sum(jnp.where(down == across, kind_ref[...], 0), axis=1, keepdims=True)
    retain = kind == 1
    target = jnp.where(retain, fr_ref[...].astype(jnp.float32), control_ref[...])
    factor = jnp.where(retain, jnp.float32(retain_weight), jnp.float32(1.0))
    out_grad = factor * (lo_ref[...].astype(jnp.float32) - target) * scale
    rows = jnp.dot(placed, out_grad, precision=lax.Precision.HIGHEST, preferred_element_type=jnp.float32)
    out_ref[...] = rows.astype(jnp.bfloat16)


def outgoing_rows(layer_out, frozen_out, control, row_kind, expert_ids, route_weights, experts_all, total_tokens):
    tokens, feats = layer_out.shape
    capacity = tokens * 3 // 8
    rows = pl.pallas_call(
        lambda *refs: rows_kernel(*refs, experts=experts_all, scale=1.0 / math.sqrt(total_tokens)),
        out_shape=jax.ShapeDtypeStruct((experts_all * capacity, feats), jnp.bfloat16),
        compiler_params=pltpu.CompilerParams(vmem_limit_bytes=60 * 2**20),
    )(layer_out, frozen_out, control[None, :], row_kind[None, :], expert_ids.T, route_weights.T)
    return rows.reshape(experts_all, capacity, feats)


def product_kernel(place_ref, slots, *refs):
    pieces, (out_ref, rows) = refs[:-2], refs[-2:]
    block = pieces[0].shape[0]

    @pl.when(pl.program_id(0) == 0)
    def _():
        rep, dp = place_ref[0], place_ref[1]
        way = jnp.where(lax.rem(rep, 2) == 0, -1, 1)
        for piece, hops in zip(pieces, (0, 1, 2, 3, 4, -1, -2, -3)):
            slot_block = lax.rem(dp + way * hops + 8, 8)
            rows[pl.ds(pl.multiple_of(slot_block * block, block), block), :] = piece[...]

    out_ref[...] = lax.dot_general(
        slots[...], rows[...], (((0,), (0,)), ((), ())), preferred_element_type=jnp.float32
    )


def product(place, slots, pieces):
    block, cols = pieces[0].shape
    width = slots.shape[1]
    in_specs = [pl.BlockSpec(memory_space=pltpu.SMEM)]
    in_specs += [pl.BlockSpec((8 * block, tile), lambda i: (0, i))]
    in_specs += [pl.BlockSpec(p.shape, lambda i: (0, 0), pipeline_mode=pl.Buffered(1)) for p in pieces]
    return pl.pallas_call(
        product_kernel,
        grid=(width // tile,),
        in_specs=in_specs,
        out_specs=pl.BlockSpec((tile, cols), lambda i: (i, 0)),
        out_shape=jax.ShapeDtypeStruct((width, cols), jnp.float32),
        scratch_shapes=[pltpu.VMEM((8 * block, cols), jnp.bfloat16)],
        compiler_params=pltpu.CompilerParams(vmem_limit_bytes=52 * 2**20),
        cost_estimate=pl.CostEstimate(
            flops=2 * 8 * block * cols * width, bytes_accessed=8 * block * (cols + width) * 2 + width * cols * 4, transcendentals=0
        ),
    )(place, slots, *pieces)


def body(layer_out, frozen_out, control, row_kind, expert_ids, route_weights, hidden):
    exp_local, slots, width = hidden.shape
    dp_count = lax.axis_size("dp")
    exp_count = lax.axis_size("expert")
    total_tokens = layer_out.shape[0] * dp_count * exp_count

    grad_send = outgoing_rows(
        layer_out, frozen_out, control, row_kind, expert_ids, route_weights, exp_local * exp_count, total_tokens
    )
    every_slot = lax.all_gather(hidden.reshape(slots, width), "rep", axis=0, tiled=True)
    mine = lax.all_to_all(grad_send, "expert", split_axis=0, concat_axis=0, tiled=True)
    mine = mine.reshape(-1, mine.shape[2])
    cores = [(i, i ^ 1) for i in range(8)]
    round_dp = [(r * 8 + d, r * 8 + (d + (1, -1)[r % 2]) % 8) for r in range(8) for d in range(8)]

    def next_dp(part):
        return lax.ppermute(part, ("rep", "dp"), round_dp)

    def other_core(part):
        return lax.ppermute(part, "rep", cores)

    ours1, pair0 = next_dp(mine), other_core(mine)
    pair1, ours2 = next_dp(pair0), next_dp(ours1)
    back1, pair2, ours3 = other_core(pair1), next_dp(pair1), next_dp(ours2)
    back2, pair3, ours4 = other_core(pair2), next_dp(pair2), next_dp(ours3)
    back3 = other_core(pair3)
    pieces = [mine, ours1, ours2, ours3, ours4, back1, back2, back3]

    place = jnp.stack([lax.axis_index("rep"), lax.axis_index("dp")]).astype(jnp.int32)
    return product(place, every_slot, pieces)[None]


def solution(mesh):
    in_specs = (
        P(("dp", "expert"), "rep"),
        P(("dp", "expert"), "rep"),
        P("rep"),
        P(("dp", "expert")),
        P(("dp", "expert"), None),
        P(("dp", "expert"), None),
        P("expert", "rep", "dp"),
    )
    out_specs = P("expert", "dp", "rep")
    return jax.shard_map(body, mesh=mesh, in_specs=in_specs, out_specs=out_specs, check_vma=False)
```

```python
import math

import jax
import jax.numpy as jnp
from jax import lax
from jax.experimental import pallas as pl
from jax.experimental.pallas import tpu as pltpu
from jax.sharding import PartitionSpec as P

retain_weight = 2.0
tile = 896


def rows_kernel(lo_ref, fr_ref, control_ref, kind_ref, ids_ref, weights_ref, out_ref, *, experts, scale):
    tokens, feats = lo_ref.shape
    capacity = out_ref.shape[0] // experts
    down = lax.broadcasted_iota(jnp.int32, (tokens, tokens), 0)
    across = lax.broadcasted_iota(jnp.int32, (tokens, tokens), 1)
    earlier = (down < across).astype(jnp.float32)
    expert = lax.broadcasted_iota(jnp.int32, (experts, tokens), 0)
    first, second = ids_ref[0:1, :] == expert, ids_ref[1:2, :] == expert
    named = (first | second).astype(jnp.float32)
    weight = jnp.where(first, weights_ref[0:1, :], 0.0) + jnp.where(second, weights_ref[1:2, :], 0.0)
    slot = jnp.dot(named, earlier, preferred_element_type=jnp.float32).astype(jnp.int32)
    slot = jnp.where(first | second, slot, -1)
    wanted = lax.broadcasted_iota(jnp.int32, (experts, capacity, tokens), 1)
    placed = jnp.where(slot[:, None, :] == wanted, weight[:, None, :], 0.0)
    placed = placed.reshape(experts * capacity, tokens)
    kind = jnp.sum(jnp.where(down == across, kind_ref[...], 0), axis=1, keepdims=True)
    retain = kind == 1
    target = jnp.where(retain, fr_ref[...].astype(jnp.float32), control_ref[...])
    factor = jnp.where(retain, jnp.float32(retain_weight), jnp.float32(1.0))
    out_grad = factor * (lo_ref[...].astype(jnp.float32) - target) * scale
    rows = jnp.dot(placed, out_grad, precision=lax.Precision.HIGHEST, preferred_element_type=jnp.float32)
    out_ref[...] = rows.astype(jnp.bfloat16)


def outgoing_rows(layer_out, frozen_out, control, row_kind, expert_ids, route_weights, experts_all, total_tokens):
    tokens, feats = layer_out.shape
    capacity = tokens * 3 // 8
    rows = pl.pallas_call(
        lambda *refs: rows_kernel(*refs, experts=experts_all, scale=1.0 / math.sqrt(total_tokens)),
        out_shape=jax.ShapeDtypeStruct((experts_all * capacity, feats), jnp.bfloat16),
        compiler_params=pltpu.CompilerParams(vmem_limit_bytes=60 * 2**20),
    )(layer_out, frozen_out, control[None, :], row_kind[None, :], expert_ids.T, route_weights.T)
    return rows.reshape(experts_all, capacity, feats)


def product_kernel(place_ref, slots, *refs):
    pieces, (out_ref, rows) = refs[:-2], refs[-2:]
    block = pieces[0].shape[0]

    @pl.when(pl.program_id(0) == 0)
    def _():
        rep, dp = place_ref[0], place_ref[1]
        way = jnp.where(lax.rem(rep, 2) == 0, -1, 1)
        for piece, hops in zip(pieces, (0, 1, 2, 3, 4, -1, -2, -3)):
            slot_block = lax.rem(dp + way * hops + 8, 8)
            rows[pl.ds(pl.multiple_of(slot_block * block, block), block), :] = piece[...]

    out_ref[...] = lax.dot_general(
        slots[...], rows[...], (((0,), (0,)), ((), ())), preferred_element_type=jnp.float32
    )


def product(place, slots, pieces):
    block, cols = pieces[0].shape
    width = slots.shape[1]
    in_specs = [pl.BlockSpec(memory_space=pltpu.SMEM)]
    in_specs += [pl.BlockSpec((8 * block, tile), lambda i: (0, i))]
    in_specs += [pl.BlockSpec(p.shape, lambda i: (0, 0), pipeline_mode=pl.Buffered(1)) for p in pieces]
    return pl.pallas_call(
        product_kernel,
        grid=(width // tile,),
        in_specs=in_specs,
        out_specs=pl.BlockSpec((tile, cols), lambda i: (i, 0)),
        out_shape=jax.ShapeDtypeStruct((width, cols), jnp.float32),
        scratch_shapes=[pltpu.VMEM((8 * block, cols), jnp.bfloat16)],
        compiler_params=pltpu.CompilerParams(vmem_limit_bytes=52 * 2**20),
        cost_estimate=pl.CostEstimate(
            flops=2 * 8 * block * cols * width, bytes_accessed=8 * block * (cols + width) * 2 + width * cols * 4, transcendentals=0
        ),
    )(place, slots, *pieces)


def body(layer_out, frozen_out, control, row_kind, expert_ids, route_weights, hidden):
    exp_local, slots, width = hidden.shape
    dp_count = lax.axis_size("dp")
    exp_count = lax.axis_size("expert")
    total_tokens = layer_out.shape[0] * dp_count * exp_count

    grad_send = outgoing_rows(
        layer_out, frozen_out, control, row_kind, expert_ids, route_weights, exp_local * exp_count, total_tokens
    )
    every_slot = lax.all_gather(hidden.reshape(slots, width), "rep", axis=0, tiled=True)
    mine = lax.all_to_all(grad_send, "expert", split_axis=0, concat_axis=0, tiled=True)
    mine = mine.reshape(-1, mine.shape[2])
    cores = [(i, i ^ 1) for i in range(8)]
    round_dp = [(r * 8 + d, r * 8 + (d + (1, -1)[r % 2]) % 8) for r in range(8) for d in range(8)]

    def next_dp(part):
        return lax.ppermute(part, ("rep", "dp"), round_dp)

    def other_core(part):
        return lax.ppermute(part, "rep", cores)

    def after(part, *earlier):
        return lax.optimization_barrier((part,) + earlier)[0]

    ours1, pair0 = next_dp(mine), other_core(mine)
    pair1, ours2 = next_dp(pair0), next_dp(ours1)
    back1 = other_core(after(pair1, ours2))
    pair2, ours3 = next_dp(pair1), next_dp(ours2)
    back2 = other_core(after(pair2, ours3))
    pair3, ours4 = next_dp(pair2), next_dp(after(ours3, back1))
    back3 = other_core(after(pair3, ours3))
    pieces = [mine, ours1, ours2, ours3, ours4, back1, back2, back3]

    place = jnp.stack([lax.axis_index("rep"), lax.axis_index("dp")]).astype(jnp.int32)
    return product(place, every_slot, pieces)[None]


def solution(mesh):
    in_specs = (
        P(("dp", "expert"), "rep"),
        P(("dp", "expert"), "rep"),
        P("rep"),
        P(("dp", "expert")),
        P(("dp", "expert"), None),
        P(("dp", "expert"), None),
        P("expert", "rep", "dp"),
    )
    out_specs = P("expert", "dp", "rep")
    return jax.shard_map(body, mesh=mesh, in_specs=in_specs, out_specs=out_specs, check_vma=False)
```

```python
import math

import jax
import jax.numpy as jnp
from jax import lax
from jax.experimental import pallas as pl
from jax.experimental.pallas import tpu as pltpu
from jax.sharding import PartitionSpec as P

retain_weight = 2.0
tile = 896


def rows_kernel(lo_ref, fr_ref, control_ref, kind_ref, ids_ref, weights_ref, out_ref, *, experts, scale):
    tokens, feats = lo_ref.shape
    capacity = out_ref.shape[0] // experts
    down = lax.broadcasted_iota(jnp.int32, (tokens, tokens), 0)
    across = lax.broadcasted_iota(jnp.int32, (tokens, tokens), 1)
    earlier = (down < across).astype(jnp.float32)
    expert = lax.broadcasted_iota(jnp.int32, (experts, tokens), 0)
    first, second = ids_ref[0:1, :] == expert, ids_ref[1:2, :] == expert
    named = (first | second).astype(jnp.float32)
    weight = jnp.where(first, weights_ref[0:1, :], 0.0) + jnp.where(second, weights_ref[1:2, :], 0.0)
    slot = jnp.dot(named, earlier, preferred_element_type=jnp.float32).astype(jnp.int32)
    slot = jnp.where(first | second, slot, -1)
    wanted = lax.broadcasted_iota(jnp.int32, (experts, capacity, tokens), 1)
    placed = jnp.where(slot[:, None, :] == wanted, weight[:, None, :], 0.0)
    placed = placed.reshape(experts * capacity, tokens)
    kind = jnp.sum(jnp.where(down == across, kind_ref[...], 0), axis=1, keepdims=True)
    retain = kind == 1
    target = jnp.where(retain, fr_ref[...].astype(jnp.float32), control_ref[...])
    factor = jnp.where(retain, jnp.float32(retain_weight), jnp.float32(1.0))
    out_grad = factor * (lo_ref[...].astype(jnp.float32) - target) * scale
    rows = jnp.dot(placed, out_grad, precision=lax.Precision.HIGHEST, preferred_element_type=jnp.float32)
    out_ref[...] = rows.astype(jnp.bfloat16)


def outgoing_rows(layer_out, frozen_out, control, row_kind, expert_ids, route_weights, experts_all, total_tokens):
    tokens, feats = layer_out.shape
    capacity = tokens * 3 // 8
    rows = pl.pallas_call(
        lambda *refs: rows_kernel(*refs, experts=experts_all, scale=1.0 / math.sqrt(total_tokens)),
        out_shape=jax.ShapeDtypeStruct((experts_all * capacity, feats), jnp.bfloat16),
        compiler_params=pltpu.CompilerParams(vmem_limit_bytes=60 * 2**20),
    )(layer_out, frozen_out, control[None, :], row_kind[None, :], expert_ids.T, route_weights.T)
    return rows.reshape(experts_all, capacity, feats)


def product_kernel(place_ref, slots, *refs):
    pieces, (out_ref, rows) = refs[:-2], refs[-2:]
    block = pieces[0].shape[0]

    @pl.when(pl.program_id(0) == 0)
    def _():
        rep, dp = place_ref[0], place_ref[1]
        way = jnp.where(lax.rem(rep, 2) == 0, -1, 1)
        for piece, hops in zip(pieces, (0, 1, 2, 3, 4, -1, -2, -3)):
            slot_block = lax.rem(dp + way * hops + 8, 8)
            rows[pl.ds(pl.multiple_of(slot_block * block, block), block), :] = piece[...]

    out_ref[...] = lax.dot_general(
        slots[...], rows[...], (((0,), (0,)), ((), ())), preferred_element_type=jnp.float32
    )


def product(place, slots, pieces):
    block, cols = pieces[0].shape
    width = slots.shape[1]
    in_specs = [pl.BlockSpec(memory_space=pltpu.SMEM)]
    in_specs += [pl.BlockSpec((8 * block, tile), lambda i: (0, i))]
    in_specs += [pl.BlockSpec(p.shape, lambda i: (0, 0), pipeline_mode=pl.Buffered(1)) for p in pieces]
    return pl.pallas_call(
        product_kernel,
        grid=(width // tile,),
        in_specs=in_specs,
        out_specs=pl.BlockSpec((tile, cols), lambda i: (i, 0)),
        out_shape=jax.ShapeDtypeStruct((width, cols), jnp.float32),
        scratch_shapes=[pltpu.VMEM((8 * block, cols), jnp.bfloat16)],
        compiler_params=pltpu.CompilerParams(vmem_limit_bytes=52 * 2**20),
        cost_estimate=pl.CostEstimate(
            flops=2 * 8 * block * cols * width, bytes_accessed=8 * block * (cols + width) * 2 + width * cols * 4, transcendentals=0
        ),
    )(place, slots, *pieces)


def body(layer_out, frozen_out, control, row_kind, expert_ids, route_weights, hidden):
    exp_local, slots, width = hidden.shape
    dp_count = lax.axis_size("dp")
    exp_count = lax.axis_size("expert")
    total_tokens = layer_out.shape[0] * dp_count * exp_count

    grad_send = outgoing_rows(
        layer_out, frozen_out, control, row_kind, expert_ids, route_weights, exp_local * exp_count, total_tokens
    )
    every_slot = lax.all_gather(hidden.reshape(slots, width), "rep", axis=0, tiled=True)
    mine = lax.all_to_all(grad_send, "expert", split_axis=0, concat_axis=0, tiled=True)
    mine = mine.reshape(-1, mine.shape[2])
    cores = [(i, i ^ 1) for i in range(8)]
    round_dp = [(r * 8 + d, r * 8 + (d + (1, -1)[r % 2]) % 8) for r in range(8) for d in range(8)]

    def next_dp(part):
        return lax.ppermute(part, ("rep", "dp"), round_dp)

    def other_core(part):
        return lax.ppermute(part, "rep", cores)

    def after(part, *earlier):
        return lax.optimization_barrier((part,) + earlier)[0]

    def crossing(part, way):
        pairs = [(r * 8 + d, (r ^ 1) * 8 + (d + (way, -way)[r % 2]) % 8) for r in range(8) for d in range(8)]
        return lax.ppermute(part, ("rep", "dp"), pairs)

    ours1, pair1 = next_dp(mine), crossing(mine, -1)
    ours2, pair2 = next_dp(ours1), next_dp(pair1)
    back1 = other_core(after(pair1, ours2))
    ours3, back3 = next_dp(ours2), crossing(pair2, 1)
    ours4 = next_dp(after(ours3, back1))
    back2 = other_core(after(pair2, ours3))
    pieces = [mine, ours1, ours2, ours3, ours4, back1, back2, back3]

    place = jnp.stack([lax.axis_index("rep"), lax.axis_index("dp")]).astype(jnp.int32)
    return product(place, every_slot, pieces)[None]


def solution(mesh):
    in_specs = (
        P(("dp", "expert"), "rep"),
        P(("dp", "expert"), "rep"),
        P("rep"),
        P(("dp", "expert")),
        P(("dp", "expert"), None),
        P(("dp", "expert"), None),
        P("expert", "rep", "dp"),
    )
    out_specs = P("expert", "dp", "rep")
    return jax.shard_map(body, mesh=mesh, in_specs=in_specs, out_specs=out_specs, check_vma=False)
```

```python
import math

import jax
import jax.numpy as jnp
from jax import lax
from jax.experimental import pallas as pl
from jax.experimental.pallas import tpu as pltpu
from jax.sharding import PartitionSpec as P

retain_weight = 2.0
tile = 896


def rows_kernel(lo_ref, fr_ref, control_ref, kind_ref, ids_ref, weights_ref, out_ref, *, experts, scale):
    tokens, feats = lo_ref.shape
    capacity = out_ref.shape[0] // experts
    down = lax.broadcasted_iota(jnp.int32, (tokens, tokens), 0)
    across = lax.broadcasted_iota(jnp.int32, (tokens, tokens), 1)
    earlier = (down < across).astype(jnp.float32)
    expert = lax.broadcasted_iota(jnp.int32, (experts, tokens), 0)
    first, second = ids_ref[0:1, :] == expert, ids_ref[1:2, :] == expert
    named = (first | second).astype(jnp.float32)
    weight = jnp.where(first, weights_ref[0:1, :], 0.0) + jnp.where(second, weights_ref[1:2, :], 0.0)
    slot = jnp.dot(named, earlier, preferred_element_type=jnp.float32).astype(jnp.int32)
    slot = jnp.where(first | second, slot, -1)
    wanted = lax.broadcasted_iota(jnp.int32, (experts, capacity, tokens), 1)
    taken = slot[:, None, :] == wanted
    scaling = jnp.sum(jnp.where(taken, weight[:, None, :], 0.0), axis=2, keepdims=True)
    scaling = scaling.reshape(experts * capacity, 1)
    chosen = jnp.where(taken, 1.0, 0.0).reshape(experts * capacity, tokens).astype(jnp.bfloat16)
    kind = jnp.sum(jnp.where(down == across, kind_ref[...], 0), axis=1, keepdims=True)
    retain = kind == 1
    target = jnp.where(retain, fr_ref[...].astype(jnp.float32), control_ref[...])
    factor = jnp.where(retain, jnp.float32(retain_weight), jnp.float32(1.0))
    out_grad = factor * (lo_ref[...].astype(jnp.float32) - target) * scale
    high = out_grad.astype(jnp.bfloat16)
    rest = out_grad - high.astype(jnp.float32)
    middle = rest.astype(jnp.bfloat16)
    low = (rest - middle.astype(jnp.float32)).astype(jnp.bfloat16)
    rows = jnp.dot(
        jnp.concatenate([chosen, chosen, chosen], axis=1),
        jnp.concatenate([high, middle, low], axis=0),
        preferred_element_type=jnp.float32,
    )
    rows = scaling * rows
    out_ref[...] = rows.astype(jnp.bfloat16)


def outgoing_rows(layer_out, frozen_out, control, row_kind, expert_ids, route_weights, experts_all, total_tokens):
    tokens, feats = layer_out.shape
    capacity = tokens * 3 // 8
    rows = pl.pallas_call(
        lambda *refs: rows_kernel(*refs, experts=experts_all, scale=1.0 / math.sqrt(total_tokens)),
        out_shape=jax.ShapeDtypeStruct((experts_all * capacity, feats), jnp.bfloat16),
        compiler_params=pltpu.CompilerParams(vmem_limit_bytes=60 * 2**20),
    )(layer_out, frozen_out, control[None, :], row_kind[None, :], expert_ids.T, route_weights.T)
    return rows.reshape(experts_all, capacity, feats)


def product_kernel(place_ref, slots, *refs):
    pieces, (out_ref, rows) = refs[:-2], refs[-2:]
    block = pieces[0].shape[0]

    @pl.when(pl.program_id(0) == 0)
    def _():
        rep, dp = place_ref[0], place_ref[1]
        way = jnp.where(lax.rem(rep, 2) == 0, -1, 1)
        for piece, hops in zip(pieces, (0, 1, 2, 3, 4, -1, -2, -3)):
            slot_block = lax.rem(dp + way * hops + 8, 8)
            rows[pl.ds(pl.multiple_of(slot_block * block, block), block), :] = piece[...]

    out_ref[...] = lax.dot_general(
        slots[...], rows[...], (((0,), (0,)), ((), ())), preferred_element_type=jnp.float32
    )


def product(place, slots, pieces):
    block, cols = pieces[0].shape
    width = slots.shape[1]
    in_specs = [pl.BlockSpec(memory_space=pltpu.SMEM)]
    in_specs += [pl.BlockSpec((8 * block, tile), lambda i: (0, i))]
    in_specs += [pl.BlockSpec(p.shape, lambda i: (0, 0), pipeline_mode=pl.Buffered(1)) for p in pieces]
    return pl.pallas_call(
        product_kernel,
        grid=(width // tile,),
        in_specs=in_specs,
        out_specs=pl.BlockSpec((tile, cols), lambda i: (i, 0)),
        out_shape=jax.ShapeDtypeStruct((width, cols), jnp.float32),
        scratch_shapes=[pltpu.VMEM((8 * block, cols), jnp.bfloat16)],
        compiler_params=pltpu.CompilerParams(vmem_limit_bytes=52 * 2**20),
        cost_estimate=pl.CostEstimate(
            flops=2 * 8 * block * cols * width, bytes_accessed=8 * block * (cols + width) * 2 + width * cols * 4, transcendentals=0
        ),
    )(place, slots, *pieces)


def body(layer_out, frozen_out, control, row_kind, expert_ids, route_weights, hidden):
    exp_local, slots, width = hidden.shape
    dp_count = lax.axis_size("dp")
    exp_count = lax.axis_size("expert")
    total_tokens = layer_out.shape[0] * dp_count * exp_count

    grad_send = outgoing_rows(
        layer_out, frozen_out, control, row_kind, expert_ids, route_weights, exp_local * exp_count, total_tokens
    )
    every_slot = lax.all_gather(hidden.reshape(slots, width), "rep", axis=0, tiled=True)
    mine = lax.all_to_all(grad_send, "expert", split_axis=0, concat_axis=0, tiled=True)
    mine = mine.reshape(-1, mine.shape[2])
    cores = [(i, i ^ 1) for i in range(8)]
    round_dp = [(r * 8 + d, r * 8 + (d + (1, -1)[r % 2]) % 8) for r in range(8) for d in range(8)]

    def next_dp(part):
        return lax.ppermute(part, ("rep", "dp"), round_dp)

    def other_core(part):
        return lax.ppermute(part, "rep", cores)

    def after(part, *earlier):
        return lax.optimization_barrier((part,) + earlier)[0]

    ours1, pair0 = next_dp(mine), other_core(mine)
    pair1, ours2 = next_dp(pair0), next_dp(ours1)
    back1 = other_core(after(pair1, ours2))
    pair2, ours3 = next_dp(pair1), next_dp(ours2)
    back2 = other_core(after(pair2, ours3))
    pair3, ours4 = next_dp(pair2), next_dp(after(ours3, back1))
    back3 = other_core(after(pair3, ours3))
    pieces = [mine, ours1, ours2, ours3, ours4, back1, back2, back3]

    place = jnp.stack([lax.axis_index("rep"), lax.axis_index("dp")]).astype(jnp.int32)
    return product(place, every_slot, pieces)[None]


def solution(mesh):
    in_specs = (
        P(("dp", "expert"), "rep"),
        P(("dp", "expert"), "rep"),
        P("rep"),
        P(("dp", "expert")),
        P(("dp", "expert"), None),
        P(("dp", "expert"), None),
        P("expert", "rep", "dp"),
    )
    out_specs = P("expert", "dp", "rep")
    return jax.shard_map(body, mesh=mesh, in_specs=in_specs, out_specs=out_specs, check_vma=False)
```

```python
import math

import jax
import jax.numpy as jnp
from jax import lax
from jax.experimental import pallas as pl
from jax.experimental.pallas import tpu as pltpu
from jax.sharding import PartitionSpec as P

retain_weight = 2.0
tile = 896


def rows_kernel(lo_ref, fr_ref, control_ref, kind_ref, ids_ref, weights_ref, out_ref, *, experts, scale):
    tokens, feats = lo_ref.shape
    capacity = out_ref.shape[0] // experts
    down = lax.broadcasted_iota(jnp.int32, (tokens, tokens), 0)
    across = lax.broadcasted_iota(jnp.int32, (tokens, tokens), 1)
    earlier = (down < across).astype(jnp.float32)
    expert = lax.broadcasted_iota(jnp.int32, (experts, tokens), 0)
    first, second = ids_ref[0:1, :] == expert, ids_ref[1:2, :] == expert
    named = (first | second).astype(jnp.float32)
    weight = jnp.where(first, weights_ref[0:1, :], 0.0) + jnp.where(second, weights_ref[1:2, :], 0.0)
    slot = jnp.dot(named, earlier, preferred_element_type=jnp.float32).astype(jnp.int32)
    slot = jnp.where(first | second, slot, -1)
    wanted = lax.broadcasted_iota(jnp.int32, (experts, capacity, tokens), 1)
    taken = slot[:, None, :] == wanted
    scaling = jnp.sum(jnp.where(taken, weight[:, None, :], 0.0), axis=2, keepdims=True)
    scaling = scaling.reshape(experts * capacity, 1)
    chosen = jnp.where(taken, 1.0, 0.0).reshape(experts * capacity, tokens).astype(jnp.bfloat16)
    kind = jnp.sum(jnp.where(down == across, kind_ref[...], 0), axis=1, keepdims=True)
    retain = kind == 1
    target = jnp.where(retain, fr_ref[...].astype(jnp.float32), control_ref[...])
    factor = jnp.where(retain, jnp.float32(retain_weight), jnp.float32(1.0))
    out_grad = factor * (lo_ref[...].astype(jnp.float32) - target) * scale
    high = out_grad.astype(jnp.bfloat16)
    rest = out_grad - high.astype(jnp.float32)
    middle = rest.astype(jnp.bfloat16)
    low = (rest - middle.astype(jnp.float32)).astype(jnp.bfloat16)
    rows = jnp.dot(
        jnp.concatenate([chosen, chosen, chosen], axis=1),
        jnp.concatenate([high, middle, low], axis=0),
        preferred_element_type=jnp.float32,
    )
    rows = scaling * rows
    out_ref[...] = rows.astype(jnp.bfloat16)


def outgoing_rows(layer_out, frozen_out, control, row_kind, expert_ids, route_weights, experts_all, total_tokens):
    tokens, feats = layer_out.shape
    capacity = tokens * 3 // 8
    rows = pl.pallas_call(
        lambda *refs: rows_kernel(*refs, experts=experts_all, scale=1.0 / math.sqrt(total_tokens)),
        out_shape=jax.ShapeDtypeStruct((experts_all * capacity, feats), jnp.bfloat16),
        compiler_params=pltpu.CompilerParams(vmem_limit_bytes=60 * 2**20),
    )(layer_out, frozen_out, control[None, :], row_kind[None, :], expert_ids.T, route_weights.T)
    return rows.reshape(experts_all, capacity, feats)


def product_kernel(place_ref, slots, *refs):
    pieces, out_ref = refs[:-1], refs[-1]
    block = pieces[0].shape[0]
    rep, dp = place_ref[0], place_ref[1]
    way = jnp.where(lax.rem(rep, 2) == 0, -1, 1)
    held = []
    for hops in (0, 1, 2, 3, 4, -1, -2, -3):
        slot_block = lax.rem(dp + way * hops + 8, 8)
        held.append(slots[pl.ds(pl.multiple_of(slot_block * block, block), block), :])
    out_ref[...] = lax.dot_general(
        jnp.concatenate(held, axis=0),
        jnp.concatenate([piece[...] for piece in pieces], axis=0),
        (((0,), (0,)), ((), ())),
        preferred_element_type=jnp.float32,
    )


def product(place, slots, pieces):
    block, cols = pieces[0].shape
    width = slots.shape[1]
    in_specs = [pl.BlockSpec(memory_space=pltpu.SMEM)]
    in_specs += [pl.BlockSpec((8 * block, tile), lambda i: (0, i))]
    in_specs += [pl.BlockSpec(p.shape, lambda i: (0, 0), pipeline_mode=pl.Buffered(1)) for p in pieces]
    return pl.pallas_call(
        product_kernel,
        grid=(width // tile,),
        in_specs=in_specs,
        out_specs=pl.BlockSpec((tile, cols), lambda i: (i, 0)),
        out_shape=jax.ShapeDtypeStruct((width, cols), jnp.float32),
        compiler_params=pltpu.CompilerParams(vmem_limit_bytes=52 * 2**20),
        cost_estimate=pl.CostEstimate(
            flops=2 * 8 * block * cols * width, bytes_accessed=8 * block * (cols + width) * 2 + width * cols * 4, transcendentals=0
        ),
    )(place, slots, *pieces)


def body(layer_out, frozen_out, control, row_kind, expert_ids, route_weights, hidden):
    exp_local, slots, width = hidden.shape
    dp_count = lax.axis_size("dp")
    exp_count = lax.axis_size("expert")
    total_tokens = layer_out.shape[0] * dp_count * exp_count

    grad_send = outgoing_rows(
        layer_out, frozen_out, control, row_kind, expert_ids, route_weights, exp_local * exp_count, total_tokens
    )
    every_slot = lax.all_gather(hidden.reshape(slots, width), "rep", axis=0, tiled=True)
    mine = lax.all_to_all(grad_send, "expert", split_axis=0, concat_axis=0, tiled=True)
    mine = mine.reshape(-1, mine.shape[2])
    cores = [(i, i ^ 1) for i in range(8)]
    round_dp = [(r * 8 + d, r * 8 + (d + (1, -1)[r % 2]) % 8) for r in range(8) for d in range(8)]

    def next_dp(part):
        return lax.ppermute(part, ("rep", "dp"), round_dp)

    def other_core(part):
        return lax.ppermute(part, "rep", cores)

    def after(part, *earlier):
        return lax.optimization_barrier((part,) + earlier)[0]

    ours1, pair0 = next_dp(mine), other_core(mine)
    pair1, ours2 = next_dp(pair0), next_dp(ours1)
    back1 = other_core(after(pair1, ours2))
    pair2, ours3 = next_dp(pair1), next_dp(ours2)
    back2 = other_core(after(pair2, ours3))
    pair3, ours4 = next_dp(pair2), next_dp(after(ours3, back1))
    back3 = other_core(after(pair3, ours3))
    pieces = [mine, ours1, ours2, ours3, ours4, back1, back2, back3]

    place = jnp.stack([lax.axis_index("rep"), lax.axis_index("dp")]).astype(jnp.int32)
    return product(place, every_slot, pieces)[None]


def solution(mesh):
    in_specs = (
        P(("dp", "expert"), "rep"),
        P(("dp", "expert"), "rep"),
        P("rep"),
        P(("dp", "expert")),
        P(("dp", "expert"), None),
        P(("dp", "expert"), None),
        P("expert", "rep", "dp"),
    )
    out_specs = P("expert", "dp", "rep")
    return jax.shard_map(body, mesh=mesh, in_specs=in_specs, out_specs=out_specs, check_vma=False)
```
